256 devices in a mesh: group: 32 (over z, x_lo, core), tensor: 8 (over y, x_hi).
Axes of the slice: x: 4 (x_hi: 2, x_lo: 2; x = x_hi * 2 + x_lo), y: 4, z: 8, core: 2. Of those that a mesh axis runs over, the one named last changes fastest.
Arguments:
- queries: bfloat16 [4, 4096, 8192], P(None, 'group', 'tensor'), may hold values from -80 to 80
- step_key_rows: bfloat16 [4, 4096, 1024], P(None, 'group', 'tensor'), may hold values from -6 to 6
- step_value_rows: bfloat16 [4, 4096, 1024], P(None, 'group', 'tensor'), may hold values from -6 to 6
- cached_key_rows: bfloat16 [4096, 32, 1024], P('group', None, 'tensor'), may hold values from -5 to 5
- cached_value_rows: bfloat16 [4096, 32, 1024], P('group', None, 'tensor'), may hold values from -6 to 6
- lengths: int32 [4096], P('group'), may hold values from 2 to 32, as said below
- output_weight: bfloat16 [8192, 4096], P('tensor'), may hold values from -0.0625 to 0.0625
- down_factor: float32 [8192, 64], P('group'), may hold values from -0.0625 to 0.0625
- up_factor: float32 [64, 4096], P(None, 'group'), may hold values from -0.75 to 0.75
Outputs:
- attended: bfloat16 [4, 4096, 4096], P(None, 'group', 'tensor')
The draws below stay inside these ranges and needn't reach their ends.
Inputs may be any that keep to these rules, and one draw needn't show every extreme that they name: `lengths`: some row holds all 32 positions.
All inputs are finite; a program needn't handle non-finite values.
Results may differ from the reference program's by a relative error of at most 0.02.
Values may be sent and summed in bfloat16 or wider, within the bound.
A program may use at most 128 MiB of HBM per device.

```python
import math
import jax
import jax.numpy as jnp
from jax import lax

OUTPUT_SLICE = 4096
QUERY_HEADS = 64
KVH = 8
HEAD_SIZE = 128
ADAPTER_RANK = 64
STEPS = 4
CACHE = 32
ROWS_ALL = 4096
N_TENSOR = 8


def shared_keys(key):
    return jnp.clip(jax.random.normal(key, (ROWS_ALL, CACHE, KVH * HEAD_SIZE), jnp.float32), -4.5, 4.5)


def draw_cached_key_rows(key, part):
    shared = shared_keys(key)
    return shared.astype(jnp.bfloat16)


def draw_queries(key, part):
    key = jax.random.fold_in(key, 23)
    values = jnp.clip(jax.random.normal(key, (STEPS, ROWS_ALL, QUERY_HEADS * HEAD_SIZE), jnp.float32), -6.0, 6.0)
    return values.astype(jnp.bfloat16)


def draw_lengths(key, part):
    key = jax.random.fold_in(key, 5)
    first_key, second_key = jax.random.split(key)
    drawn = jax.random.randint(first_key, (ROWS_ALL,), 2, CACHE + 1)
    chosen = jax.random.randint(second_key, (), 0, ROWS_ALL)
    return jnp.where(jnp.arange(ROWS_ALL) == chosen, CACHE, drawn).astype(jnp.int32)


def block_levels(stream_key, shape, cuts, smallest, top_value):
    def one(dim, blocks):
        draws = jax.random.uniform(jax.random.fold_in(jax.random.fold_in(stream_key, 6), dim), (blocks,), jnp.float32, smallest / len(cuts), top_value / len(cuts))
        return jnp.repeat(jnp.exp(draws), shape[dim] // blocks).reshape((-1,) + (1,) * (len(shape) - dim - 1))

    factor_of = one(*cuts[0])
    for cut in cuts[1:]:
        factor_of = factor_of * one(*cut)
    return factor_of


def normal_values(own_key, shape, deviation, reach, cuts=(), dtype=jnp.bfloat16):
    loudness = block_levels(own_key, shape, cuts, -0.22, 0.18) if cuts else 1.0
    entries = jax.random.normal(own_key, shape, jnp.float32) * deviation * loudness
    return jnp.minimum(jnp.maximum(entries, -reach), reach).astype(dtype)


def setup_inputs(seed: int = 0) -> dict:
    seeds = jax.random.split(jax.random.key(seed), 10)
    return {
        "queries": draw_queries(jax.random.fold_in(seeds[9], 71), 0),
        "step_key_rows": normal_values(seeds[1], (STEPS, ROWS_ALL, KVH * HEAD_SIZE), 1.0, 6.0, ((1, 32), (2, 8))),
        "step_value_rows": normal_values(seeds[2], (STEPS, ROWS_ALL, KVH * HEAD_SIZE), 1.0, 6.0, ((1, 32), (2, 8))),
        "cached_key_rows": draw_cached_key_rows(jax.random.fold_in(seeds[9], 71), 0),
        "cached_value_rows": normal_values(seeds[4], (ROWS_ALL, CACHE, KVH * HEAD_SIZE), 1.0, 6.0, ((0, 32), (2, 8))),
        "lengths": draw_lengths(jax.random.fold_in(seeds[9], 71), 0),
        "output_weight": normal_values(seeds[6], (QUERY_HEADS * HEAD_SIZE, OUTPUT_SLICE), (QUERY_HEADS * HEAD_SIZE) ** -0.5, 0.0625, ((0, 8),)),
        "down_factor": normal_values(seeds[7], (QUERY_HEADS * HEAD_SIZE, ADAPTER_RANK), (QUERY_HEADS * HEAD_SIZE) ** -0.5, 0.0625, ((0, 32),), jnp.float32),
        "up_factor": normal_values(seeds[8], (ADAPTER_RANK, OUTPUT_SLICE), ADAPTER_RANK ** -0.5, 0.75, ((1, 32),), jnp.float32),
    }


adapter_scale = 2.0

def attend(query, cache_k, cache_v, fresh_k, fresh_v, lengths):
    row_count = query.shape[0]
    kv_heads = cache_k.shape[2] // HEAD_SIZE
    group_size = QUERY_HEADS // KVH
    cache_len = cache_k.shape[1]
    query_h = query.reshape(row_count, kv_heads, group_size, HEAD_SIZE).astype(jnp.float32)
    keys_c = cache_k.reshape(row_count, cache_len, kv_heads, HEAD_SIZE).astype(jnp.float32)
    values_c = cache_v.reshape(row_count, cache_len, kv_heads, HEAD_SIZE).astype(jnp.float32)
    keys_n = fresh_k.reshape(fresh_k.shape[0], row_count, kv_heads, HEAD_SIZE).astype(jnp.float32)
    values_n = fresh_v.reshape(fresh_v.shape[0], row_count, kv_heads, HEAD_SIZE).astype(jnp.float32)
    inverse_root = 1.0 / math.sqrt(HEAD_SIZE)
    cache_scores = jnp.einsum('rkgd,rckd->rkgc', query_h, keys_c) * inverse_root
    in_cache = lax.broadcasted_iota(jnp.int32, (row_count, 1, 1, cache_len), 3) < lengths.reshape(row_count, 1, 1, 1)
    cache_scores = jnp.where(in_cache, cache_scores, -jnp.inf)
    fresh_scores = jnp.einsum('rkgd,trkd->rkgt', query_h, keys_n) * inverse_root
    row_max = jnp.maximum(lax.optimization_barrier(jnp.max(cache_scores, axis=-1, keepdims=True)), lax.optimization_barrier(jnp.max(fresh_scores, axis=-1, keepdims=True)))
    cache_exp = jnp.exp(cache_scores - row_max)
    fresh_exp = jnp.exp(fresh_scores - row_max)
    denominator = lax.optimization_barrier(jnp.sum(cache_exp, axis=-1, keepdims=True)) + lax.optimization_barrier(jnp.sum(fresh_exp, axis=-1, keepdims=True))
    cache_weights = (cache_exp / denominator).astype(jnp.bfloat16).astype(jnp.float32)
    fresh_weights = (fresh_exp / denominator).astype(jnp.bfloat16).astype(jnp.float32)
    attention_context = jnp.einsum('rkgc,rckd->rkgd', cache_weights, values_c) + jnp.einsum('rkgt,trkd->rkgd', fresh_weights, values_n)
    return attention_context.reshape(row_count, kv_heads * group_size * HEAD_SIZE).astype(jnp.bfloat16)

def reference(queries, step_key_rows, step_value_rows, cached_key_rows, cached_value_rows, lengths, output_weight, down_factor, up_factor):
    contexts = []
    for step_index in range(STEPS):
        contexts.append(attend(queries[step_index], cached_key_rows, cached_value_rows, step_key_rows[:step_index + 1], step_value_rows[:step_index + 1], lengths))
    attention_context = jnp.stack(contexts).reshape(STEPS * ROWS_ALL, QUERY_HEADS * HEAD_SIZE)
    head_width = QUERY_HEADS * HEAD_SIZE // N_TENSOR
    base_sum = jnp.zeros((STEPS * ROWS_ALL, OUTPUT_SLICE), jnp.float32)
    for shard in range(N_TENSOR):
        partial_term = jnp.dot(attention_context[:, shard * head_width:(shard + 1) * head_width], output_weight[shard * head_width:(shard + 1) * head_width], preferred_element_type=jnp.float32)
        rounded = lax.optimization_barrier(partial_term.astype(jnp.bfloat16))
        base_sum = base_sum + rounded.astype(jnp.float32)
    rank_projected = jnp.dot(attention_context.astype(jnp.float32), down_factor, precision=lax.Precision.HIGHEST)
    adapter_output = adapter_scale * jnp.dot(rank_projected, up_factor, precision=lax.Precision.HIGHEST)
    return (base_sum + adapter_output).astype(jnp.bfloat16).reshape(STEPS, ROWS_ALL, OUTPUT_SLICE)
```

```python
import functools
import math

import jax
import jax.numpy as jnp
from jax import lax
from jax.experimental import pallas as pl
from jax.experimental.pallas import tpu as pltpu
from jax.sharding import PartitionSpec as P

MESH = pl.DeviceIdType.MESH
BF = jnp.bfloat16
F32 = jnp.float32

STEPS = 4
ROWS = 128
HEADS = 8
D = 128
CACHE = 32
WIDTH = HEADS * D
COLS = 512
HALF = COLS // 2
CHUNK = 32
CHUNKS = ROWS // CHUNK
M = STEPS * CHUNK
ADAPTER_SCALE = 2.0
NEG = -1e30
EXP2_SCALE = math.log2(math.e) / math.sqrt(D)

TREE2 = {
    (1, 1): (0, 1),
    (2, 1): (3, 1),
    (0, 1): (0, 0),
    (3, 1): (3, 0),
    (2, 0): (1, 0),
    (1, 0): (0, 0),
    (3, 0): (0, 0),
}


def mirror(tree):
    flip = lambda n: ((4 - n[0]) % 4, n[1])
    return {flip(a): flip(b) for a, b in tree.items()}


def children(tree, node):
    return [a for a, b in tree.items() if b == node]


def level(tree, node):
    kids = children(tree, node)
    return 0 if not kids else 1 + max(level(tree, k) for k in kids)


def trees_of(chunk):
    return (TREE2, mirror(TREE2))


NODES = [(r, o) for r in (2, 1, 3, 0) for o in (1, 0)]
EDGES = [n for n in NODES if n != (0, 0)]


def block_order():
    trees = trees_of(0)
    items = [(level(trees[h], n), i, h, n) for i, n in enumerate(NODES) for h in (0, 1)]
    items.sort(key=lambda t: (t[0], t[1], t[2]))
    return [(n, h) for _, _, h, n in items]


BLOCKS = block_order()
BLOCK_INDEX = {b: i for i, b in enumerate(BLOCKS)}
EDGE_INDEX = {(n, h): 2 * i + h for i, n in enumerate(EDGES) for h in (0, 1)}


def kernel(
    q_ref, ks_ref, vs_ref, kc_ref, vc_ref, len_ref, w_ref, d_ref, u_ref, o_ref,
    q_v, ks_v, vs_v, kc_v, vc_v, w_v, d_v, u_v, ctx_v, part_v, recv_v, fac_v, proj_v, prcv_v, out_v,
    in_sem, w_sem, send_sem, recv_sem, zsend_sem, zrecv_sem, qsend_sem, qrecv_sem, psend_sem, precv_sem, out_sem,
):
    g = lax.axis_index("group")
    t = lax.axis_index("tensor")
    z, quad = g // 4, g % 4
    y, xh = t // 2, t % 2
    dev = lambda gg, yy, xx: (gg, yy * 2 + xx)
    y_up = dev(g, (y + 1) % 4, xh)
    y_down = dev(g, (y + 3) % 4, xh)
    x_peer = dev(g, y, 1 - xh)
    z_peers = [(((z + k) % 8) * 4 + quad, t) for k in range(1, 8)]
    quad_ids = [(quad + k) % 4 for k in range(1, 4)]
    quad_peers = [(z * 4 + k, t) for k in quad_ids]

    barrier = pltpu.get_barrier_semaphore()
    peers = [y_up, y_down, x_peer] + z_peers + quad_peers
    for p in peers:
        pl.semaphore_signal(barrier, inc=1, device_id=p, device_id_type=MESH)

    def fetch(src, dst, sem):
        c = pltpu.make_async_copy(src, dst, sem)
        c.start()
        return c

    first = pl.ds(0, CHUNK)
    rest = pl.ds(CHUNK, ROWS - CHUNK)
    loads = []
    for k, rows in enumerate((first, rest)):
        loads.append([
            fetch(q_ref.at[:, rows, :], q_v.at[:, rows, :], in_sem.at[k, 0]),
            fetch(kc_ref.at[rows], kc_v.at[rows], in_sem.at[k, 1]),
            fetch(vc_ref.at[rows], vc_v.at[rows], in_sem.at[k, 2]),
        ])
        if k == 0:
            loads[0] += [
                fetch(ks_ref, ks_v, in_sem.at[k, 3]),
                fetch(vs_ref, vs_v, in_sem.at[k, 4]),
            ]
            fac_loads = [
                fetch(d_ref, d_v, in_sem.at[1, 3]),
                fetch(u_ref, u_v, in_sem.at[1, 4]),
            ]

            w_loads = []

            def load_w(i):
                (r, o), h = BLOCKS[i]
                dest = ((y + 4 - r) % 4) * 2 + ((xh + o) % 2)
                cols = pl.ds(pl.multiple_of(dest * COLS + h * HALF, HALF), HALF)
                w_loads.append(fetch(w_ref.at[:, cols], w_v.at[i], w_sem.at[i]))

            for i in range(6):
                load_w(i)
    for i in range(6, len(BLOCKS)):
        load_w(i)

    def attention(chunk):
        row0 = chunk * CHUNK
        ks_c = ks_v[:, row0:row0 + CHUNK, :].reshape(STEPS * CHUNK, D)
        vs_c = vs_v[:, row0:row0 + CHUNK, :].reshape(STEPS * CHUNK, D)
        ones = jnp.ones((STEPS * CHUNK, D), BF)
        vs_ext = jnp.concatenate([vs_c, ones], axis=1)
        sub = lax.broadcasted_iota(jnp.int32, (8, 2 * D), 0)
        lane = lax.broadcasted_iota(jnp.int32, (8, 2 * D), 1)

        def sixteen(jj, carry):
            r0 = pl.multiple_of(row0 + jj * 16, 16)
            qf = q_v[:, pl.ds(r0, 16), :].astype(F32)
            outs = []
            for part in range(2):
                qb = jnp.concatenate(
                    [
                        qf[s, part * 8:part * 8 + 8, h * D:(h + 1) * D]
                        for s in range(STEPS)
                        for h in range(HEADS)
                    ],
                    axis=0,
                ).astype(BF)
                rp = r0 + part * 8
                k8 = kc_v[pl.ds(rp, 8)].reshape(8 * CACHE, D)
                v8 = vc_v[pl.ds(rp, 8)].reshape(8 * CACHE, D)
                contract = (((1,), (1,)), ((), ()))
                s1 = lax.dot_general(qb, k8, contract, preferred_element_type=F32)
                s2 = lax.dot_general(qb, ks_c, contract, preferred_element_type=F32)
                lens = jnp.zeros((8, 2 * D), jnp.int32)
                for i in range(8):
                    lens = jnp.where(sub == i, len_ref[rp + i], lens)
                ok1 = (lane // CACHE == sub) & (lane % CACHE < lens)
                bias1 = jnp.where(ok1, 0.0, NEG).astype(F32)
                sub2, lane2 = sub[:, :D], lane[:, :D]
                mine = lane2 % CHUNK == sub2 + (jj * 16 + part * 8)
                bias2 = jnp.stack(
                    [
                        jnp.where(mine & (lane2 // CHUNK <= s), 0.0, NEG).astype(F32)
                        for s in range(STEPS)
                    ]
                )
                s1 = s1.reshape(STEPS * HEADS, 8, 2 * D) + bias1[None]
                s2 = s2.reshape(STEPS, HEADS, 8, D) + bias2[:, None]
                s1 = s1.reshape(STEPS * HEADS * 8, 2 * D)
                s2 = s2.reshape(STEPS * HEADS * 8, D)
                top = jnp.maximum(jnp.maximum(s1[:, :D], s1[:, D:]), s2)
                top = jnp.max(top, axis=1, keepdims=True)
                p1 = jnp.exp2((s1 - top) * EXP2_SCALE).astype(BF)
                p2 = jnp.exp2((s2 - top) * EXP2_SCALE).astype(BF)
                v_ext = jnp.concatenate([v8, jnp.ones((8 * CACHE, D), BF)], axis=1)
                acc = jnp.dot(p1, v_ext, preferred_element_type=F32) + jnp.dot(
                    p2, vs_ext, preferred_element_type=F32
                )
                outs.append(acc[:, :D] / acc[:, D:])
            for s in range(STEPS):
                for h in range(HEADS):
                    i = (s * HEADS + h) * 8
                    tile = jnp.concatenate([outs[0][i:i + 8], outs[1][i:i + 8]], axis=0)
                    ctx_v[chunk, pl.ds(pl.multiple_of(s * CHUNK + jj * 16, 16), 16), h * D:(h + 1) * D] = (
                        tile.astype(BF)
                    )
            return carry

        lax.fori_loop(0, CHUNK // 16, sixteen, 0)

    def product(chunk, b):
        i = BLOCK_INDEX[b]
        if chunk == 0:
            w_loads[i].wait()
        part_v[chunk, i] = jnp.dot(ctx_v[chunk], w_v[i], preferred_element_type=F32).astype(BF)

    sends = []

    def target_of(node, parent):
        if node[1] != parent[1]:
            return x_peer
        return y_up if (parent[0] - node[0]) % 4 == 1 else y_down

    def edge_copy(chunk, node, h):
        e = EDGE_INDEX[(node, h)]
        parent = trees_of(chunk)[h][node]
        return pltpu.make_async_remote_copy(
            src_ref=part_v.at[chunk, BLOCK_INDEX[(node, h)]],
            dst_ref=recv_v.at[chunk, e],
            send_sem=send_sem.at[chunk, e],
            recv_sem=recv_sem.at[chunk, e],
            device_id=target_of(node, parent),
            device_id_type=MESH,
        )

    def send(chunk, node, h):
        c = edge_copy(chunk, node, h)
        c.start()
        sends.append(c)

    def combine(chunk, node, h):
        i = BLOCK_INDEX[(node, h)]
        total = part_v[chunk, i].astype(F32)
        for kid in children(trees_of(chunk)[h], node):
            edge_copy(chunk, kid, h).wait_recv()
            total = total + recv_v[chunk, EDGE_INDEX[(kid, h)]].astype(F32)
        part_v[chunk, i] = total.astype(BF)
        send(chunk, node, h)

    def at_level(chunk, lv):
        trees = trees_of(chunk)
        return [(n, h) for n, h in BLOCKS if n != (0, 0) and level(trees[h], n) == lv]

    owner = z == t
    z_copies = [
        pltpu.make_async_remote_copy(
            src_ref=fac_v.at[quad], dst_ref=fac_v.at[quad],
            send_sem=zsend_sem.at[k], recv_sem=zrecv_sem.at[0],
            device_id=z_peers[k], device_id_type=MESH,
        )
        for k in range(7)
    ]
    quad_copies = [
        pltpu.make_async_remote_copy(
            src_ref=fac_v.at[quad], dst_ref=fac_v.at[quad],
            send_sem=qsend_sem.at[k], recv_sem=qrecv_sem.at[2 - k],
            device_id=quad_peers[k], device_id_type=MESH,
        )
        for k in range(3)
    ]

    def factors_out():
        for c in fac_loads:
            c.wait()

        @pl.when(owner)
        def _():
            fac_v[quad, 0:D, :] = jnp.concatenate([d_v[0:D, :], d_v[D:2 * D, :]], axis=1).astype(BF)
            fac_v[quad, D:D + 64, :] = u_v[...].astype(BF)
            for c in z_copies:
                c.start()

    def factors_quad():
        @pl.when(jnp.logical_not(owner))
        def _():
            z_copies[0].wait_recv()

        for c in quad_copies:
            c.start()

    def factors_wait():
        for c in quad_copies:
            c.wait_recv()

    lane_m = lax.broadcasted_iota(jnp.int32, (2 * M, D), 1)

    def project():
        halves = []
        for k in range(2):
            lo = jnp.zeros((2 * M, D), F32)
            hi = jnp.zeros((2 * M, D), F32)
            ctx = ctx_v[2 * k:2 * k + 2].reshape(2 * M, WIDTH)
            for j in range(4):
                f = fac_v[j, 0:D, :]
                lo = lo + jnp.dot(ctx[:, 2 * j * D:(2 * j + 1) * D], f, preferred_element_type=F32)
                hi = hi + jnp.dot(ctx[:, (2 * j + 1) * D:(2 * j + 2) * D], f, preferred_element_type=F32)
            if k == 0:
                halves.append(lo + pltpu.roll(hi, 64, 1))
            else:
                halves.append(hi + pltpu.roll(lo, 64, 1))
        proj_v[0] = jnp.where(lane_m < 64, halves[0], halves[1]).astype(BF)

    y_pair = dev(g, y + 1 - 2 * (y % 2), xh)
    y_flip = dev(g, 3 - y, xh)
    p_copies = [
        pltpu.make_async_remote_copy(
            src_ref=proj_v.at[k], dst_ref=prcv_v.at[k],
            send_sem=psend_sem.at[k], recv_sem=precv_sem.at[k],
            device_id=p, device_id_type=MESH,
        )
        for k, p in enumerate((x_peer, y_pair, y_flip))
    ]

    def proj_step(k):
        p_copies[k].wait_recv()
        proj_v[k + 1] = (proj_v[k].astype(F32) + prcv_v[k].astype(F32)).astype(BF)
        if k < 2:
            p_copies[k + 1].start()

    outs = []

    def finish(chunk):
        proj = proj_v[3, pl.ds((chunk % 2) * M, M), :]
        lane = lax.broadcasted_iota(jnp.int32, (M, D), 1)
        keep = lane < 64 if chunk < 2 else lane >= 64
        proj = jnp.where(keep, proj.astype(F32) * ADAPTER_SCALE, 0.0).astype(BF)
        for h in range(2):
            total = part_v[chunk, BLOCK_INDEX[((0, 0), h)]].astype(F32)
            for kid in children(trees_of(chunk)[h], (0, 0)):
                edge_copy(chunk, kid, h).wait_recv()
                total = total + recv_v[chunk, EDGE_INDEX[(kid, h)]].astype(F32)
            for j in range(2):
                u = fac_v[2 * h + j, D:D + 64, :]
                low = jnp.dot(proj, jnp.concatenate([u, u], axis=0), preferred_element_type=F32)
                res = (total[:, j * D:(j + 1) * D] + low).astype(BF)
                out_v[:, chunk * CHUNK:(chunk + 1) * CHUNK, h * HALF + j * D:h * HALF + (j + 1) * D] = (
                    res.reshape(STEPS, CHUNK, D)
                )
        rows = pl.ds(chunk * CHUNK, CHUNK)
        outs.append(fetch(out_v.at[:, rows, :], o_ref.at[:, rows, :], out_sem.at[chunk]))

    for chunk in range(CHUNKS):
        if chunk < 2:
            for c in loads[chunk]:
                c.wait()
        attention(chunk)
        if chunk == 0:
            pl.semaphore_wait(barrier, len(peers))
            factors_out()
        trees = trees_of(chunk)
        for n, h in BLOCKS:
            product(chunk, (n, h))
            if level(trees[h], n) == 0:
                send(chunk, n, h)
        if chunk == 1:
            factors_quad()
        if chunk >= 1:
            for n, h in at_level(chunk - 1, 1):
                combine(chunk - 1, n, h)
    factors_wait()
    project()
    p_copies[0].start()
    last = CHUNKS - 1
    for n, h in at_level(last, 1):
        combine(last, n, h)
    for chunk in range(CHUNKS):
        for n, h in at_level(chunk, 2):
            combine(chunk, n, h)
        if chunk < 3:
            proj_step(chunk)
    for chunk in range(CHUNKS):
        finish(chunk)

    for c in sends:
        c.wait_send()

    @pl.when(owner)
    def _():
        for c in z_copies:
            c.wait_send()

    for c in quad_copies + p_copies:
        c.wait_send()
    for c in outs:
        c.wait()


def body(q, ks, vs, kc, vc, lengths, w, d, u):
    any_spec = pl.BlockSpec(memory_space=pl.ANY)
    smem = pl.BlockSpec(memory_space=pltpu.SMEM)
    dma = pltpu.SemaphoreType.DMA
    return pl.pallas_call(
        kernel,
        out_shape=jax.ShapeDtypeStruct((STEPS, ROWS, COLS), BF),
        in_specs=[any_spec] * 5 + [smem] + [any_spec] * 3,
        out_specs=any_spec,
        scratch_shapes=[
            pltpu.VMEM((STEPS, ROWS, WIDTH), BF),
            pltpu.VMEM((STEPS, ROWS, D), BF),
            pltpu.VMEM((STEPS, ROWS, D), BF),
            pltpu.VMEM((ROWS, CACHE, D), BF),
            pltpu.VMEM((ROWS, CACHE, D), BF),
            pltpu.VMEM((16, WIDTH, HALF), BF),
            pltpu.VMEM((256, 64), F32),
            pltpu.VMEM((64, 128), F32),
            pltpu.VMEM((CHUNKS, M, WIDTH), BF),
            pltpu.VMEM((CHUNKS, 16, M, HALF), BF),
            pltpu.VMEM((CHUNKS, 14, M, HALF), BF),
            pltpu.VMEM((4, D + 64, D), BF),
            pltpu.VMEM((4, 2 * M, D), BF),
            pltpu.VMEM((3, 2 * M, D), BF),
            pltpu.VMEM((STEPS, ROWS, COLS), BF),
            dma((2, 5)),
            dma((16,)),
            dma((CHUNKS, 14)),
            dma((CHUNKS, 14)),
            dma((7,)),
            dma((1,)),
            dma((3,)),
            dma((3,)),
            dma((3,)),
            dma((3,)),
            dma((CHUNKS,)),
        ],
        compiler_params=pltpu.CompilerParams(
            collective_id=1, has_side_effects=True, vmem_limit_bytes=48 << 20
        ),
        cost_estimate=pl.CostEstimate(
            flops=2 * 512 * 1024 * 4200, bytes_accessed=13 << 20, transcendentals=1 << 20
        ),
        name="attend_project_reduce",
    )(q, ks, vs, kc, vc, lengths, w, d, u)


def solution(mesh):
    return jax.shard_map(
        body,
        mesh=mesh,
        in_specs=(
            P(None, "group", "tensor"),
            P(None, "group", "tensor"),
            P(None, "group", "tensor"),
            P("group", None, "tensor"),
            P("group", None, "tensor"),
            P("group"),
            P("tensor", None),
            P("group", None),
            P(None, "group"),
        ),
        out_specs=P(None, "group", "tensor"),
        check_vma=False,
    )
```

```python
import functools
import math

import jax
import jax.numpy as jnp
from jax import lax
from jax.experimental import pallas as pl
from jax.experimental.pallas import tpu as pltpu
from jax.sharding import PartitionSpec as P

MESH = pl.DeviceIdType.MESH
BF = jnp.bfloat16
F32 = jnp.float32

STEPS = 4
ROWS = 128
HEADS = 8
D = 128
CACHE = 32
WIDTH = HEADS * D
COLS = 512
HALF = COLS // 2
GROUP = 32
CHUNK_ROWS = (32, 32, 32, 32)
CHUNK_TREES = (3, 1, 3, 2)
ROW0 = [sum(CHUNK_ROWS[:c]) for c in range(len(CHUNK_ROWS))]
CHUNKS = len(CHUNK_ROWS)
ADAPTER_SCALE = 2.0
NEG = -1e30
EXP2_SCALE = math.log2(math.e) / math.sqrt(D)

TREES = {
    1: {(2, 1): (1, 1), (1, 1): (0, 1), (3, 1): (0, 1), (0, 1): (0, 0), (2, 0): (1, 0), (1, 0): (0, 0), (3, 0): (0, 0)},
    2: {(1, 1): (0, 1), (2, 1): (3, 1), (0, 1): (0, 0), (3, 1): (3, 0), (2, 0): (1, 0), (1, 0): (0, 0), (3, 0): (0, 0)},
    3: {(1, 1): (0, 1), (2, 1): (2, 0), (3, 1): (3, 0), (0, 1): (0, 0), (2, 0): (1, 0), (1, 0): (0, 0), (3, 0): (0, 0)},
    4: {(1, 1): (1, 0), (2, 1): (2, 0), (3, 1): (3, 0), (0, 1): (0, 0), (2, 0): (1, 0), (1, 0): (0, 0), (3, 0): (0, 0)},
}


def mirror(tree):
    flip = lambda n: ((4 - n[0]) % 4, n[1])
    return {flip(a): flip(b) for a, b in tree.items()}


def trees_of(chunk):
    tree = TREES[CHUNK_TREES[chunk]]
    return (tree, mirror(tree))


def children(tree, node):
    return [a for a, b in tree.items() if b == node]


NODES = [(r, o) for r in (2, 1, 3, 0) for o in (1, 0)]
ROOT = (0, 0)
EDGE_INDEX = {(n, h): 2 * i + h for i, n in enumerate(NODES[:-1]) for h in (0, 1)}

ORDER = (
    "A0", "O", "L0210", "L0211", "L0110", "L0310", "L0111", "L0311", "A1", "L1210", "L1211", "L1200", "L1310",
    "L1201", "L1111", "L1300", "C0200", "C0010", "L1101", "C0011", "A2", "C0201", "C0300", "C1110", "C1311",
    "L2210", "C1100", "Q", "L2211", "L2110", "C0101", "L2310", "L2111", "L2311", "M0100", "M0301", "C1301",
    "M0000", "M0001", "M1010", "M1011", "M1000", "M1001", "M2200", "M2201", "C0100", "M2100", "M2300", "M2010",
    "M2101", "M2301", "M2011", "M2000", "M2001", "A3", "C0301", "C1010", "C2200", "L3210", "L3211", "L3200",
    "L3110", "L3201", "L3311", "M3310", "P", "C1011", "M3111", "M3100", "M3300", "M3010", "M3101", "M3301",
    "C2201", "C2010", "C2011", "M3011", "M3000", "M3001", "C2300", "C2101", "C2100", "C3310", "R", "C3111",
    "C3301", "C3100", "C3011", "C3010", "C2301", "C3300", "R", "C3101", "R", "F0", "F1", "F2", "F3",
)
STEPS_IN_ORDER = [(w[0], tuple(int(x) for x in w[1:])) for w in ORDER]


def block_order():
    seen = []
    for kind, v in STEPS_IN_ORDER:
        if kind in "LMC":
            b = ((v[1], v[2]), v[3])
            if b not in seen:
                seen.append(b)
        elif kind == "F":
            for b in ((ROOT, 0), (ROOT, 1)):
                if b not in seen:
                    seen.append(b)
    return seen


BLOCKS = block_order()
BLOCK_INDEX = {b: i for i, b in enumerate(BLOCKS)}


def kernel(
    q_ref, ks_ref, vs_ref, kc_ref, vc_ref, len_ref, w_ref, d_ref, u_ref, o_ref,
    q_v, ks_v, vs_v, kc_v, vc_v, w_v, len_v, d_v, u_v, ctx_v, part_v, recv_v, fac_v, proj_v, prcv_v, out_v,
    in_sem, w_sem, send_sem, recv_sem, zsend_sem, zrecv_sem, qsend_sem, qrecv_sem, psend_sem, precv_sem, out_sem,
):
    g = lax.axis_index("group")
    t = lax.axis_index("tensor")
    z, quad = g // 4, g % 4
    y, xh = t // 2, t % 2
    dev = lambda gg, yy, xx: (gg, yy * 2 + xx)
    y_up = dev(g, (y + 1) % 4, xh)
    y_down = dev(g, (y + 3) % 4, xh)
    x_peer = dev(g, y, 1 - xh)
    z_peers = [(((z + k) % 8) * 4 + quad, t) for k in range(1, 8)]
    quad_ids = [(quad + k) % 4 for k in range(1, 4)]
    quad_peers = [(z * 4 + k, t) for k in quad_ids]

    contract = (((1,), (1,)), ((), ()))
    barrier = pltpu.get_barrier_semaphore()
    peers = [y_up, y_down, x_peer] + z_peers + quad_peers
    for p in peers:
        pl.semaphore_signal(barrier, inc=1, device_id=p, device_id_type=MESH)

    def fetch(src, dst, sem):
        c = pltpu.make_async_copy(src, dst, sem)
        c.start()
        return c

    loads = []
    w_loads = []

    def load_rows(k, lo, hi):
        rows = pl.ds(lo, hi - lo)
        loads.append([
            fetch(q_ref.at[:, rows, :], q_v.at[:, rows, :], in_sem.at[k, 0]),
            fetch(kc_ref.at[rows], kc_v.at[rows], in_sem.at[k, 1]),
            fetch(vc_ref.at[rows], vc_v.at[rows], in_sem.at[k, 2]),
        ])

    def load_w(i):
        (r, o), h = BLOCKS[i]
        dest = ((y + 4 - r) % 4) * 2 + ((xh + o) % 2)
        cols = pl.ds(pl.multiple_of(dest * COLS + h * HALF, HALF), HALF)
        w_loads.append(fetch(w_ref.at[:, cols], w_v.at[i], w_sem.at[i]))

    fac_loads = [fetch(d_ref, d_v, in_sem.at[0, 3]), fetch(u_ref, u_v, in_sem.at[0, 4])]
    load_rows(0, 0, 16)
    loads[0] += [
        fetch(ks_ref.at[:, 0:GROUP, :], ks_v.at[:, 0:GROUP, :], in_sem.at[1, 3]),
        fetch(vs_ref.at[:, 0:GROUP, :], vs_v.at[:, 0:GROUP, :], in_sem.at[1, 4]),
        fetch(len_ref, len_v, in_sem.at[0, 5]),
    ]
    load_rows(1, 16, GROUP)
    for i in range(6):
        load_w(i)
    def later_loads():
        load_rows(2, GROUP, ROWS)
        loads[2].extend([
            fetch(ks_ref.at[:, GROUP:, :], ks_v.at[:, GROUP:, :], in_sem.at[2, 3]),
            fetch(vs_ref.at[:, GROUP:, :], vs_v.at[:, GROUP:, :], in_sem.at[2, 4]),
        ])
        for i in range(6, len(BLOCKS)):
            load_w(i)

    waited = set()

    def loaded(k):
        if k not in waited:
            waited.add(k)
            for c in loads[k]:
                c.wait()

    def attention(chunk):
        loaded(0 if chunk == 0 else 2)
        row0, rows = ROW0[chunk], CHUNK_ROWS[chunk]
        g0 = row0 // GROUP * GROUP
        ks_c = ks_v[:, g0:g0 + GROUP, :].reshape(STEPS * GROUP, D)
        vs_c = vs_v[:, g0:g0 + GROUP, :].reshape(STEPS * GROUP, D)
        ones = jnp.ones((STEPS * GROUP, D), BF)
        vs_ext = jnp.concatenate([vs_c, ones], axis=1)
        sub = lax.broadcasted_iota(jnp.int32, (8, 2 * D), 0)
        lane = lax.broadcasted_iota(jnp.int32, (8, 2 * D), 1)

        def sixteen(jj, carry):
            r0 = pl.multiple_of(row0 + jj * 16, 16)
            qf = q_v[:, pl.ds(r0, 16), :].astype(F32)
            outs = []
            for part in range(2):
                qb = jnp.concatenate(
                    [
                        qf[s, part * 8:part * 8 + 8, h * D:(h + 1) * D]
                        for s in range(STEPS)
                        for h in range(HEADS)
                    ],
                    axis=0,
                ).astype(BF)
                rp = r0 + part * 8
                k8 = kc_v[pl.ds(rp, 8)].reshape(8 * CACHE, D)
                v8 = vc_v[pl.ds(rp, 8)].reshape(8 * CACHE, D)
                s1 = lax.dot_general(qb, k8, contract, preferred_element_type=F32)
                s2 = lax.dot_general(qb, ks_c, contract, preferred_element_type=F32)
                lens = jnp.zeros((8, 2 * D), jnp.int32)
                for i in range(8):
                    lens = jnp.where(sub == i, len_v[rp + i], lens)
                ok1 = (lane // CACHE == sub) & (lane % CACHE < lens)
                bias1 = jnp.where(ok1, 0.0, NEG).astype(F32)
                sub2, lane2 = sub[:, :D], lane[:, :D]
                mine = lane2 % GROUP == sub2 + (rp - g0)
                bias2 = jnp.stack(
                    [
                        jnp.where(mine & (lane2 // GROUP <= s), 0.0, NEG).astype(F32)
                        for s in range(STEPS)
                    ]
                )
                s1 = s1.reshape(STEPS * HEADS, 8, 2 * D) + bias1[None]
                s2 = s2.reshape(STEPS, HEADS, 8, D) + bias2[:, None]
                s1 = s1.reshape(STEPS * HEADS * 8, 2 * D)
                s2 = s2.reshape(STEPS * HEADS * 8, D)
                top = jnp.maximum(jnp.maximum(s1[:, :D], s1[:, D:]), s2)
                top = jnp.max(top, axis=1, keepdims=True)
                p1 = jnp.exp2((s1 - top) * EXP2_SCALE).astype(BF)
                p2 = jnp.exp2((s2 - top) * EXP2_SCALE).astype(BF)
                v_ext = jnp.concatenate([v8, jnp.ones((8 * CACHE, D), BF)], axis=1)
                acc = jnp.dot(p1, v_ext, preferred_element_type=F32) + jnp.dot(
                    p2, vs_ext, preferred_element_type=F32
                )
                outs.append(acc[:, :D] / acc[:, D:])
            for s in range(STEPS):
                for h in range(HEADS):
                    i = (s * HEADS + h) * 8
                    tile = jnp.concatenate([outs[0][i:i + 8], outs[1][i:i + 8]], axis=0)
                    at = pl.multiple_of(STEPS * row0 + s * rows + jj * 16, 16)
                    ctx_v[pl.ds(at, 16), h * D:(h + 1) * D] = tile.astype(BF)
            return carry

        if chunk == 0:
            for jj in range(rows // 16):
                loaded(jj)
                sixteen(jj, 0)
                if jj == 0:
                    later_loads()
        else:
            lax.fori_loop(0, rows // 16, sixteen, 0)

    def span(chunk):
        return pl.ds(STEPS * ROW0[chunk], STEPS * CHUNK_ROWS[chunk])

    multiplied = set()
    fetched = set()

    def product(chunk, b):
        if (chunk, b) in multiplied:
            return
        multiplied.add((chunk, b))
        i = BLOCK_INDEX[b]
        if i not in fetched:
            fetched.add(i)
            w_loads[i].wait()
        part_v[i, span(chunk), :] = jnp.dot(
            ctx_v[span(chunk), :], w_v[i], preferred_element_type=F32
        ).astype(BF)

    sends = []

    def target_of(node, parent):
        if node[1] != parent[1]:
            return x_peer
        return y_up if (parent[0] - node[0]) % 4 == 1 else y_down

    def edge_copy(chunk, node, h):
        e = EDGE_INDEX[(node, h)]
        parent = trees_of(chunk)[h][node]
        return pltpu.make_async_remote_copy(
            src_ref=part_v.at[BLOCK_INDEX[(node, h)], span(chunk), :],
            dst_ref=recv_v.at[e, span(chunk), :],
            send_sem=send_sem.at[chunk, e],
            recv_sem=recv_sem.at[chunk, e],
            device_id=target_of(node, parent),
            device_id_type=MESH,
        )

    def send(chunk, node, h):
        c = edge_copy(chunk, node, h)
        c.start()
        sends.append(c)

    def gathered(chunk, node, h):
        total = part_v[BLOCK_INDEX[(node, h)], span(chunk), :].astype(F32)
        for kid in children(trees_of(chunk)[h], node):
            edge_copy(chunk, kid, h).wait_recv()
            total = total + recv_v[EDGE_INDEX[(kid, h)], span(chunk), :].astype(F32)
        return total

    def combine(chunk, node, h):
        i = BLOCK_INDEX[(node, h)]
        part_v[i, span(chunk), :] = gathered(chunk, node, h).astype(BF)
        send(chunk, node, h)

    owner = z == t
    z_copies = [
        pltpu.make_async_remote_copy(
            src_ref=fac_v.at[quad], dst_ref=fac_v.at[quad],
            send_sem=zsend_sem.at[k], recv_sem=zrecv_sem.at[0],
            device_id=z_peers[k], device_id_type=MESH,
        )
        for k in range(7)
    ]
    quad_copies = [
        pltpu.make_async_remote_copy(
            src_ref=fac_v.at[quad], dst_ref=fac_v.at[quad],
            send_sem=qsend_sem.at[k], recv_sem=qrecv_sem.at[2 - k],
            device_id=quad_peers[k], device_id_type=MESH,
        )
        for k in range(3)
    ]

    def factors_out():
        for c in fac_loads:
            c.wait()

        @pl.when(owner)
        def _():
            fac_v[quad, 0:D, :] = jnp.concatenate([d_v[:, 0:D], d_v[:, D:2 * D]], axis=0).astype(BF)
            fac_v[quad, D:D + 64, :] = u_v[...].astype(BF)
            for c in z_copies:
                c.start()

    def factors_quad():
        @pl.when(jnp.logical_not(owner))
        def _():
            z_copies[0].wait_recv()

        for c in quad_copies:
            c.start()

    def factors_wait():
        for c in quad_copies:
            c.wait_recv()

    half_m = STEPS * ROWS // 2
    lane_m = lax.broadcasted_iota(jnp.int32, (half_m, D), 1)

    def project():
        halves = []
        for k in range(2):
            lo = jnp.zeros((half_m, D), F32)
            hi = jnp.zeros((half_m, D), F32)
            ctx = ctx_v[k * half_m:(k + 1) * half_m, :]
            for j in range(4):
                f = fac_v[j, 0:D, :]
                lo = lo + lax.dot_general(
                    ctx[:, 2 * j * D:(2 * j + 1) * D], f, contract, preferred_element_type=F32
                )
                hi = hi + lax.dot_general(
                    ctx[:, (2 * j + 1) * D:(2 * j + 2) * D], f, contract, preferred_element_type=F32
                )
            if k == 0:
                halves.append(lo + pltpu.roll(hi, 64, 1))
            else:
                halves.append(hi + pltpu.roll(lo, 64, 1))
        proj_v[0] = jnp.where(lane_m < 64, halves[0], halves[1]).astype(BF)

    y_pair = dev(g, y + 1 - 2 * (y % 2), xh)
    y_flip = dev(g, 3 - y, xh)
    p_copies = [
        pltpu.make_async_remote_copy(
            src_ref=proj_v.at[k], dst_ref=prcv_v.at[k],
            send_sem=psend_sem.at[k], recv_sem=precv_sem.at[k],
            device_id=p, device_id_type=MESH,
        )
        for k, p in enumerate((x_peer, y_pair, y_flip))
    ]

    def proj_step(k):
        p_copies[k].wait_recv()
        proj_v[k + 1] = (proj_v[k].astype(F32) + prcv_v[k].astype(F32)).astype(BF)
        if k < 2:
            p_copies[k + 1].start()

    outs = []

    def finish(chunk):
        rows, m0 = CHUNK_ROWS[chunk], STEPS * ROW0[chunk]
        m = STEPS * rows
        proj = proj_v[3, pl.ds(m0 % half_m, m), :]
        lane = lax.broadcasted_iota(jnp.int32, (m, D), 1)
        keep = lane < 64 if m0 < half_m else lane >= 64
        proj = jnp.where(keep, proj.astype(F32) * ADAPTER_SCALE, 0.0).astype(BF)
        row_span = pl.ds(ROW0[chunk], rows)
        for h in range(2):
            total = gathered(chunk, ROOT, h)
            for j in range(2):
                u = fac_v[2 * h + j, D:D + 64, :]
                low = jnp.dot(proj, jnp.concatenate([u, u], axis=0), preferred_element_type=F32)
                res = (total[:, j * D:(j + 1) * D] + low).astype(BF)
                out_v[:, row_span, h * HALF + j * D:h * HALF + (j + 1) * D] = res.reshape(STEPS, rows, D)
        outs.append(fetch(out_v.at[:, row_span, :], o_ref.at[:, row_span, :], out_sem.at[chunk]))

    ar_steps = 0
    greeted = False
    for kind, v in STEPS_IN_ORDER:
        if kind in "LO" and not greeted:
            greeted = True
            pl.semaphore_wait(barrier, len(peers))
        if kind == "A":
            attention(v[0])
        elif kind == "O":
            factors_out()
        elif kind in "LMC":
            chunk, node, h = v[0], (v[1], v[2]), v[3]
            product(chunk, (node, h))
            if kind == "L":
                send(chunk, node, h)
            elif kind == "C":
                combine(chunk, node, h)
        elif kind == "F":
            for h in (0, 1):
                product(v[0], (ROOT, h))
            finish(v[0])
        elif kind == "Q":
            factors_quad()
        elif kind == "P":
            factors_wait()
            project()
            p_copies[0].start()
        else:
            proj_step(ar_steps)
            ar_steps += 1

    for c in sends:
        c.wait_send()

    @pl.when(owner)
    def _():
        for c in z_copies:
            c.wait_send()

    for c in quad_copies + p_copies:
        c.wait_send()
    for c in outs:
        c.wait()


def body(q, ks, vs, kc, vc, lengths, w, d, u):
    hbm = pl.BlockSpec(memory_space=pltpu.HBM)
    dma = pltpu.SemaphoreType.DMA
    return pl.pallas_call(
        kernel,
        out_shape=jax.ShapeDtypeStruct((STEPS, ROWS, COLS), BF),
        in_specs=[hbm] * 9,
        out_specs=hbm,
        scratch_shapes=[
            pltpu.VMEM((STEPS, ROWS, WIDTH), BF),
            pltpu.VMEM((STEPS, ROWS, D), BF),
            pltpu.VMEM((STEPS, ROWS, D), BF),
            pltpu.VMEM((ROWS, CACHE, D), BF),
            pltpu.VMEM((ROWS, CACHE, D), BF),
            pltpu.VMEM((16, WIDTH, HALF), BF),
            pltpu.SMEM((ROWS,), jnp.int32),
            pltpu.VMEM((64, 256), F32),
            pltpu.VMEM((64, 128), F32),
            pltpu.VMEM((STEPS * ROWS, WIDTH), BF),
            pltpu.VMEM((16, STEPS * ROWS, HALF), BF),
            pltpu.VMEM((14, STEPS * ROWS, HALF), BF),
            pltpu.VMEM((4, D + 64, D), BF),
            pltpu.VMEM((4, STEPS * ROWS // 2, D), BF),
            pltpu.VMEM((3, STEPS * ROWS // 2, D), BF),
            pltpu.VMEM((STEPS, ROWS, COLS), BF),
            dma((3, 6)),
            dma((16,)),
            dma((CHUNKS, 14)),
            dma((CHUNKS, 14)),
            dma((7,)),
            dma((1,)),
            dma((3,)),
            dma((3,)),
            dma((3,)),
            dma((3,)),
            dma((CHUNKS,)),
        ],
        compiler_params=pltpu.CompilerParams(
            collective_id=1, has_side_effects=True, vmem_limit_bytes=64 << 20
        ),
        cost_estimate=pl.CostEstimate(
            flops=2 * 512 * 1024 * 4200, bytes_accessed=13 << 20, transcendentals=1 << 20
        ),
        name="attend_project_reduce",
    )(q, ks, vs, kc, vc, lengths, w, d.T, u)


def solution(mesh):
    return jax.shard_map(
        body,
        mesh=mesh,
        in_specs=(
            P(None, "group", "tensor"),
            P(None, "group", "tensor"),
            P(None, "group", "tensor"),
            P("group", None, "tensor"),
            P("group", None, "tensor"),
            P("group"),
            P("tensor", None),
            P("group", None),
            P(None, "group"),
        ),
        out_specs=P(None, "group", "tensor"),
        check_vma=False,
    )
```

```python
import functools
import math

import jax
import jax.numpy as jnp
from jax import lax
from jax.experimental import pallas as pl
from jax.experimental.pallas import tpu as pltpu
from jax.sharding import PartitionSpec as P

MESH = pl.DeviceIdType.MESH
BF = jnp.bfloat16
F32 = jnp.float32

STEPS = 4
ROWS = 128
HEADS = 8
D = 128
CACHE = 32
WIDTH = HEADS * D
COLS = 512
HALF = COLS // 2
GROUP = 32
CHUNK_ROWS = (32, 32, 32, 32)
CHUNK_TREES = (3, 1, 3, 2)
ROW0 = [sum(CHUNK_ROWS[:c]) for c in range(len(CHUNK_ROWS))]
CHUNKS = len(CHUNK_ROWS)
ADAPTER_SCALE = 2.0
NEG = -1e30
EXP2_SCALE = math.log2(math.e) / math.sqrt(D)

TREES = {
    1: {(2, 1): (1, 1), (1, 1): (0, 1), (3, 1): (0, 1), (0, 1): (0, 0), (2, 0): (1, 0), (1, 0): (0, 0), (3, 0): (0, 0)},
    2: {(1, 1): (0, 1), (2, 1): (3, 1), (0, 1): (0, 0), (3, 1): (3, 0), (2, 0): (1, 0), (1, 0): (0, 0), (3, 0): (0, 0)},
    3: {(1, 1): (0, 1), (2, 1): (2, 0), (3, 1): (3, 0), (0, 1): (0, 0), (2, 0): (1, 0), (1, 0): (0, 0), (3, 0): (0, 0)},
    4: {(1, 1): (1, 0), (2, 1): (2, 0), (3, 1): (3, 0), (0, 1): (0, 0), (2, 0): (1, 0), (1, 0): (0, 0), (3, 0): (0, 0)},
}


def mirror(tree):
    flip = lambda n: ((4 - n[0]) % 4, n[1])
    return {flip(a): flip(b) for a, b in tree.items()}


def trees_of(chunk):
    tree = TREES[CHUNK_TREES[chunk]]
    return (tree, mirror(tree))


def children(tree, node):
    return [a for a, b in tree.items() if b == node]


NODES = [(r, o) for r in (2, 1, 3, 0) for o in (1, 0)]
ROOT = (0, 0)
EDGE_INDEX = {(n, h): 2 * i + h for i, n in enumerate(NODES[:-1]) for h in (0, 1)}

ORDER = (
    "A0", "O", "L0210", "L0211", "L0110", "L0310", "L0111", "L0311", "A1", "L1210", "L1211", "L1200", "L1310",
    "L1201", "L1111", "L1300", "C0200", "C0010", "L1101", "C0011", "A2", "Q", "C0201", "C0300", "C1110", "C1311",
    "L2210", "C1100", "L2211", "L2110", "C0101", "L2310", "L2111", "L2311", "M0100", "M0301", "C1301", "M0000",
    "M0001", "M1010", "M1011", "M1000", "M1001", "M2200", "M2201", "C0100", "M2100", "M2300", "M2010", "M2101",
    "M2301", "M2011", "M2000", "M2001", "A3", "C0301", "C1010", "C2200", "L3210", "L3211", "L3200", "L3110",
    "L3201", "L3311", "M3310", "C1011", "M3111", "M3100", "M3300", "M3010", "M3101", "M3301", "P", "C2201",
    "C2010", "C2011", "M3011", "M3000", "M3001", "C2300", "C2101", "C2100", "C3310", "R", "C3111", "C3301",
    "C3100", "C3011", "C3010", "C2301", "C3300", "R", "C3101", "R", "F0", "F1", "F2", "F3",
)
STEPS_IN_ORDER = [(w[0], tuple(int(x) for x in w[1:])) for w in ORDER]


def block_order():
    seen = []
    for kind, v in STEPS_IN_ORDER:
        if kind in "LMC":
            b = ((v[1], v[2]), v[3])
            if b not in seen:
                seen.append(b)
        elif kind == "F":
            for b in ((ROOT, 0), (ROOT, 1)):
                if b not in seen:
                    seen.append(b)
    return seen


BLOCKS = block_order()
BLOCK_INDEX = {b: i for i, b in enumerate(BLOCKS)}


def kernel(
    q_ref, ks_ref, vs_ref, kc_ref, vc_ref, len_ref, w_ref, d_ref, u_ref, o_ref,
    q_v, ks_v, vs_v, kc_v, vc_v, w_v, len_v, d_v, u_v, ctx_v, part_v, recv_v, fac_v, proj_v, prcv_v,
    in_sem, w_sem, send_sem, recv_sem, zsend_sem, zrecv_sem, qsend_sem, qrecv_sem, psend_sem, precv_sem,
):
    g = lax.axis_index("group")
    t = lax.axis_index("tensor")
    z, quad = g // 4, g % 4
    y, xh = t // 2, t % 2
    dev = lambda gg, yy, xx: (gg, yy * 2 + xx)
    y_up = dev(g, (y + 1) % 4, xh)
    y_down = dev(g, (y + 3) % 4, xh)
    x_peer = dev(g, y, 1 - xh)
    z_peers = [(((z + k) % 8) * 4 + quad, t) for k in range(1, 8)]
    quad_ids = [(quad + k) % 4 for k in range(1, 4)]
    quad_peers = [(z * 4 + k, t) for k in quad_ids]

    contract = (((1,), (1,)), ((), ()))
    barrier = pltpu.get_barrier_semaphore()
    peers = [y_up, y_down, x_peer] + z_peers + quad_peers
    for p in peers:
        pl.semaphore_signal(barrier, inc=1, device_id=p, device_id_type=MESH)

    def fetch(src, dst, sem):
        c = pltpu.make_async_copy(src, dst, sem)
        c.start()
        return c

    loads = []
    w_loads = []

    def load_rows(k, lo, hi):
        rows = pl.ds(lo, hi - lo)
        loads.append([
            fetch(q_ref.at[:, rows, :], q_v.at[:, rows, :], in_sem.at[k, 0]),
            fetch(kc_ref.at[rows], kc_v.at[rows], in_sem.at[k, 1]),
            fetch(vc_ref.at[rows], vc_v.at[rows], in_sem.at[k, 2]),
        ])

    def load_w(i):
        (r, o), h = BLOCKS[i]
        dest = ((y + 4 - r) % 4) * 2 + ((xh + o) % 2)
        cols = pl.ds(pl.multiple_of(dest * COLS + h * HALF, HALF), HALF)
        w_loads.append(fetch(w_ref.at[:, cols], w_v.at[i], w_sem.at[i]))

    fac_loads = [fetch(d_ref, d_v, in_sem.at[0, 3]), fetch(u_ref, u_v, in_sem.at[0, 4])]
    load_rows(0, 0, 16)
    loads[0] += [
        fetch(ks_ref.at[:, 0:GROUP, :], ks_v.at[:, 0:GROUP, :], in_sem.at[1, 3]),
        fetch(vs_ref.at[:, 0:GROUP, :], vs_v.at[:, 0:GROUP, :], in_sem.at[1, 4]),
        fetch(len_ref, len_v, in_sem.at[0, 5]),
    ]
    load_rows(1, 16, GROUP)
    for i in range(6):
        load_w(i)
    def later_loads():
        load_rows(2, GROUP, ROWS)
        loads[2].extend([
            fetch(ks_ref.at[:, GROUP:, :], ks_v.at[:, GROUP:, :], in_sem.at[2, 3]),
            fetch(vs_ref.at[:, GROUP:, :], vs_v.at[:, GROUP:, :], in_sem.at[2, 4]),
        ])
        for i in range(6, len(BLOCKS)):
            load_w(i)

    waited = set()

    def loaded(k):
        if k not in waited:
            waited.add(k)
            for c in loads[k]:
                c.wait()

    def attention(chunk):
        loaded(0 if chunk == 0 else 2)
        row0, rows = ROW0[chunk], CHUNK_ROWS[chunk]
        g0 = row0 // GROUP * GROUP
        ks_c = ks_v[:, g0:g0 + GROUP, :].reshape(STEPS * GROUP, D)
        vs_c = vs_v[:, g0:g0 + GROUP, :].reshape(STEPS * GROUP, D)
        ones = jnp.ones((STEPS * GROUP, D), BF)
        vs_ext = jnp.concatenate([vs_c, ones], axis=1)
        sub = lax.broadcasted_iota(jnp.int32, (8, 2 * D), 0)
        lane = lax.broadcasted_iota(jnp.int32, (8, 2 * D), 1)

        def sixteen(jj, carry):
            r0 = pl.multiple_of(row0 + jj * 16, 16)
            qf = q_v[:, pl.ds(r0, 16), :].astype(F32)
            outs = []
            for part in range(2):
                qb = jnp.concatenate(
                    [
                        qf[s, part * 8:part * 8 + 8, h * D:(h + 1) * D]
                        for s in range(STEPS)
                        for h in range(HEADS)
                    ],
                    axis=0,
                ).astype(BF)
                rp = r0 + part * 8
                k8 = kc_v[pl.ds(rp, 8)].reshape(8 * CACHE, D)
                v8 = vc_v[pl.ds(rp, 8)].reshape(8 * CACHE, D)
                s1 = lax.dot_general(qb, k8, contract, preferred_element_type=F32)
                s2 = lax.dot_general(qb, ks_c, contract, preferred_element_type=F32)
                lens = jnp.zeros((8, 2 * D), jnp.int32)
                for i in range(8):
                    lens = jnp.where(sub == i, len_v[rp + i], lens)
                ok1 = (lane // CACHE == sub) & (lane % CACHE < lens)
                bias1 = jnp.where(ok1, 0.0, NEG).astype(F32)
                sub2, lane2 = sub[:, :D], lane[:, :D]
                mine = lane2 % GROUP == sub2 + (rp - g0)
                bias2 = jnp.stack(
                    [
                        jnp.where(mine & (lane2 // GROUP <= s), 0.0, NEG).astype(F32)
                        for s in range(STEPS)
                    ]
                )
                s1 = s1.reshape(STEPS * HEADS, 8, 2 * D) + bias1[None]
                s2 = s2.reshape(STEPS, HEADS, 8, D) + bias2[:, None]
                s1 = s1.reshape(STEPS * HEADS * 8, 2 * D)
                s2 = s2.reshape(STEPS * HEADS * 8, D)
                top = jnp.maximum(jnp.maximum(s1[:, :D], s1[:, D:]), s2)
                top = jnp.max(top, axis=1, keepdims=True)
                p1 = jnp.exp2((s1 - top) * EXP2_SCALE).astype(BF)
                p2 = jnp.exp2((s2 - top) * EXP2_SCALE).astype(BF)
                v_ext = jnp.concatenate([v8, jnp.ones((8 * CACHE, D), BF)], axis=1)
                acc = jnp.dot(p1, v_ext, preferred_element_type=F32) + jnp.dot(
                    p2, vs_ext, preferred_element_type=F32
                )
                outs.append(acc[:, :D] / acc[:, D:])
            for s in range(STEPS):
                for h in range(HEADS):
                    i = (s * HEADS + h) * 8
                    tile = jnp.concatenate([outs[0][i:i + 8], outs[1][i:i + 8]], axis=0)
                    at = pl.multiple_of(STEPS * row0 + s * rows + jj * 16, 16)
                    ctx_v[pl.ds(at, 16), h * D:(h + 1) * D] = tile.astype(BF)
            return carry

        if chunk == 0:
            for jj in range(rows // 16):
                loaded(jj)
                sixteen(jj, 0)
                if jj == 0:
                    later_loads()
        else:
            lax.fori_loop(0, rows // 16, sixteen, 0)

    def span(chunk):
        return pl.ds(STEPS * ROW0[chunk], STEPS * CHUNK_ROWS[chunk])

    multiplied = set()
    fetched = set()

    def product(chunk, b):
        if (chunk, b) in multiplied:
            return
        multiplied.add((chunk, b))
        i = BLOCK_INDEX[b]
        if i not in fetched:
            fetched.add(i)
            w_loads[i].wait()
        part_v[i, span(chunk), :] = jnp.dot(
            ctx_v[span(chunk), :], w_v[i], preferred_element_type=F32
        ).astype(BF)

    sends = []

    def target_of(node, parent):
        if node[1] != parent[1]:
            return x_peer
        return y_up if (parent[0] - node[0]) % 4 == 1 else y_down

    def edge_copy(chunk, node, h):
        e = EDGE_INDEX[(node, h)]
        parent = trees_of(chunk)[h][node]
        return pltpu.make_async_remote_copy(
            src_ref=part_v.at[BLOCK_INDEX[(node, h)], span(chunk), :],
            dst_ref=recv_v.at[e, span(chunk), :],
            send_sem=send_sem.at[chunk, e],
            recv_sem=recv_sem.at[chunk, e],
            device_id=target_of(node, parent),
            device_id_type=MESH,
        )

    def send(chunk, node, h):
        c = edge_copy(chunk, node, h)
        c.start()
        sends.append(c)

    def gathered(chunk, node, h):
        total = part_v[BLOCK_INDEX[(node, h)], span(chunk), :].astype(F32)
        for kid in children(trees_of(chunk)[h], node):
            edge_copy(chunk, kid, h).wait_recv()
            total = total + recv_v[EDGE_INDEX[(kid, h)], span(chunk), :].astype(F32)
        return total

    def combine(chunk, node, h):
        i = BLOCK_INDEX[(node, h)]
        part_v[i, span(chunk), :] = gathered(chunk, node, h).astype(BF)
        send(chunk, node, h)

    owner = z == t
    parts = [fac_v.at[quad, pl.ds(0, D), :], fac_v.at[quad, pl.ds(D, 64), :]]
    z_copies = [
        [
            pltpu.make_async_remote_copy(
                src_ref=part, dst_ref=part,
                send_sem=zsend_sem.at[k, i], recv_sem=zrecv_sem.at[i],
                device_id=z_peers[k], device_id_type=MESH,
            )
            for k in range(7)
        ]
        for i, part in enumerate(parts)
    ]
    quad_copies = [
        [
            pltpu.make_async_remote_copy(
                src_ref=part, dst_ref=part,
                send_sem=qsend_sem.at[k, i], recv_sem=qrecv_sem.at[2 - k, i],
                device_id=quad_peers[k], device_id_type=MESH,
            )
            for k in range(3)
        ]
        for i, part in enumerate(parts)
    ]

    def factors_out():
        for c in fac_loads:
            c.wait()

        @pl.when(owner)
        def _():
            fac_v[quad, 0:D, :] = jnp.concatenate([d_v[:, 0:D], d_v[:, D:2 * D]], axis=0).astype(BF)
            fac_v[quad, D:D + 64, :] = u_v[...].astype(BF)
            for c in z_copies[0] + z_copies[1]:
                c.start()

    def factors_quad(i):
        @pl.when(jnp.logical_not(owner))
        def _():
            z_copies[i][0].wait_recv()

        for c in quad_copies[i]:
            c.start()

    def factors_wait(i):
        for c in quad_copies[i]:
            c.wait_recv()

    half_m = STEPS * ROWS // 2
    lane_m = lax.broadcasted_iota(jnp.int32, (half_m, D), 1)

    def project():
        halves = []
        for k in range(2):
            lo = jnp.zeros((half_m, D), F32)
            hi = jnp.zeros((half_m, D), F32)
            ctx = ctx_v[k * half_m:(k + 1) * half_m, :]
            for j in range(4):
                f = fac_v[j, 0:D, :]
                lo = lo + lax.dot_general(
                    ctx[:, 2 * j * D:(2 * j + 1) * D], f, contract, preferred_element_type=F32
                )
                hi = hi + lax.dot_general(
                    ctx[:, (2 * j + 1) * D:(2 * j + 2) * D], f, contract, preferred_element_type=F32
                )
            if k == 0:
                halves.append(lo + pltpu.roll(hi, 64, 1))
            else:
                halves.append(hi + pltpu.roll(lo, 64, 1))
        proj_v[0] = jnp.where(lane_m < 64, halves[0], halves[1]).astype(BF)

    y_pair = dev(g, y + 1 - 2 * (y % 2), xh)
    y_flip = dev(g, 3 - y, xh)
    p_copies = [
        pltpu.make_async_remote_copy(
            src_ref=proj_v.at[k], dst_ref=prcv_v.at[k],
            send_sem=psend_sem.at[k], recv_sem=precv_sem.at[k],
            device_id=p, device_id_type=MESH,
        )
        for k, p in enumerate((x_peer, y_pair, y_flip))
    ]

    def proj_step(k):
        p_copies[k].wait_recv()
        proj_v[k + 1] = (proj_v[k].astype(F32) + prcv_v[k].astype(F32)).astype(BF)
        if k < 2:
            p_copies[k + 1].start()

    def finish(chunk):
        rows, m0 = CHUNK_ROWS[chunk], STEPS * ROW0[chunk]
        m = STEPS * rows
        proj = proj_v[3, pl.ds(m0 % half_m, m), :]
        lane = lax.broadcasted_iota(jnp.int32, (m, D), 1)
        keep = lane < 64 if m0 < half_m else lane >= 64
        proj = jnp.where(keep, proj.astype(F32) * ADAPTER_SCALE, 0.0).astype(BF)
        row_span = pl.ds(ROW0[chunk], rows)
        for h in range(2):
            total = gathered(chunk, ROOT, h)
            for j in range(2):
                u = fac_v[2 * h + j, D:D + 64, :]
                low = jnp.dot(proj, jnp.concatenate([u, u], axis=0), preferred_element_type=F32)
                res = (total[:, j * D:(j + 1) * D] + low).astype(BF)
                o_ref[:, row_span, h * HALF + j * D:h * HALF + (j + 1) * D] = res.reshape(STEPS, rows, D)

    ar_steps = finished = 0
    greeted = False
    for kind, v in STEPS_IN_ORDER:
        if kind in "LO" and not greeted:
            greeted = True
            pl.semaphore_wait(barrier, len(peers))
        if kind == "A":
            attention(v[0])
        elif kind == "O":
            factors_out()
        elif kind in "LMC":
            chunk, node, h = v[0], (v[1], v[2]), v[3]
            product(chunk, (node, h))
            if kind == "L":
                send(chunk, node, h)
            elif kind == "C":
                combine(chunk, node, h)
        elif kind == "F":
            for h in (0, 1):
                product(v[0], (ROOT, h))
            if not finished:
                factors_wait(1)
            finished += 1
            finish(v[0])
        elif kind == "Q":
            factors_quad(0)
        elif kind == "P":
            factors_wait(0)
            project()
            p_copies[0].start()
            factors_quad(1)
        else:
            proj_step(ar_steps)
            ar_steps += 1

    for c in sends:
        c.wait_send()

    @pl.when(owner)
    def _():
        for c in z_copies[0] + z_copies[1]:
            c.wait_send()

    for c in quad_copies[0] + quad_copies[1] + p_copies:
        c.wait_send()


def body(q, ks, vs, kc, vc, lengths, w, d, u):
    hbm = pl.BlockSpec(memory_space=pltpu.HBM)
    dma = pltpu.SemaphoreType.DMA
    return pl.pallas_call(
        kernel,
        out_shape=pltpu.VMEM((STEPS, ROWS, COLS), BF),
        in_specs=[hbm] * 9,
        out_specs=pl.BlockSpec(memory_space=pltpu.VMEM),
        scratch_shapes=[
            pltpu.VMEM((STEPS, ROWS, WIDTH), BF),
            pltpu.VMEM((STEPS, ROWS, D), BF),
            pltpu.VMEM((STEPS, ROWS, D), BF),
            pltpu.VMEM((ROWS, CACHE, D), BF),
            pltpu.VMEM((ROWS, CACHE, D), BF),
            pltpu.VMEM((16, WIDTH, HALF), BF),
            pltpu.SMEM((ROWS,), jnp.int32),
            pltpu.VMEM((64, 256), F32),
            pltpu.VMEM((64, 128), F32),
            pltpu.VMEM((STEPS * ROWS, WIDTH), BF),
            pltpu.VMEM((16, STEPS * ROWS, HALF), BF),
            pltpu.VMEM((14, STEPS * ROWS, HALF), BF),
            pltpu.VMEM((4, D + 64, D), BF),
            pltpu.VMEM((4, STEPS * ROWS // 2, D), BF),
            pltpu.VMEM((3, STEPS * ROWS // 2, D), BF),
            dma((3, 6)),
            dma((16,)),
            dma((CHUNKS, 14)),
            dma((CHUNKS, 14)),
            dma((7, 2)),
            dma((2,)),
            dma((3, 2)),
            dma((3, 2)),
            dma((3,)),
            dma((3,)),
        ],
        compiler_params=pltpu.CompilerParams(
            collective_id=1, has_side_effects=True, vmem_limit_bytes=54 << 20
        ),
        cost_estimate=pl.CostEstimate(
            flops=2 * 512 * 1024 * 4200, bytes_accessed=13 << 20, transcendentals=1 << 20
        ),
        name="attend_project_reduce",
    )(q, ks, vs, kc, vc, lengths, w, d.T, u)


def solution(mesh):
    return jax.shard_map(
        body,
        mesh=mesh,
        in_specs=(
            P(None, "group", "tensor"),
            P(None, "group", "tensor"),
            P(None, "group", "tensor"),
            P("group", None, "tensor"),
            P("group", None, "tensor"),
            P("group"),
            P("tensor", None),
            P("group", None),
            P(None, "group"),
        ),
        out_specs=P(None, "group", "tensor"),
        check_vma=False,
    )
```

```python
import functools
import math

import jax
import jax.numpy as jnp
from jax import lax
from jax.experimental import pallas as pl
from jax.experimental.pallas import tpu as pltpu
from jax.sharding import PartitionSpec as P

MESH = pl.DeviceIdType.MESH
BF = jnp.bfloat16
F32 = jnp.float32

STEPS = 4
ROWS = 128
HEADS = 8
D = 128
CACHE = 32
WIDTH = HEADS * D
COLS = 512
HALF = COLS // 2
GROUP = 32
CHUNK_ROWS = (32, 32, 32, 32)
CHUNK_TREES = (3, 1, 3, 2)
ROW0 = [sum(CHUNK_ROWS[:c]) for c in range(len(CHUNK_ROWS))]
CHUNKS = len(CHUNK_ROWS)
ADAPTER_SCALE = 2.0
NEG = -1e30
EXP2_SCALE = math.log2(math.e) / math.sqrt(D)

TREES = {
    1: {(2, 1): (1, 1), (1, 1): (0, 1), (3, 1): (0, 1), (0, 1): (0, 0), (2, 0): (1, 0), (1, 0): (0, 0), (3, 0): (0, 0)},
    2: {(1, 1): (0, 1), (2, 1): (3, 1), (0, 1): (0, 0), (3, 1): (3, 0), (2, 0): (1, 0), (1, 0): (0, 0), (3, 0): (0, 0)},
    3: {(1, 1): (0, 1), (2, 1): (2, 0), (3, 1): (3, 0), (0, 1): (0, 0), (2, 0): (1, 0), (1, 0): (0, 0), (3, 0): (0, 0)},
    4: {(1, 1): (1, 0), (2, 1): (2, 0), (3, 1): (3, 0), (0, 1): (0, 0), (2, 0): (1, 0), (1, 0): (0, 0), (3, 0): (0, 0)},
}


def mirror(tree):
    flip = lambda n: ((4 - n[0]) % 4, n[1])
    return {flip(a): flip(b) for a, b in tree.items()}


def trees_of(chunk):
    tree = TREES[CHUNK_TREES[chunk]]
    return (tree, mirror(tree))


def children(tree, node):
    return [a for a, b in tree.items() if b == node]


NODES = [(r, o) for r in (2, 1, 3, 0) for o in (1, 0)]
ROOT = (0, 0)
EDGE_INDEX = {(n, h): 2 * i + h for i, n in enumerate(NODES[:-1]) for h in (0, 1)}

ORDER = (
    "A0", "O", "L0210", "L0211", "L0110", "L0310", "L0111", "L0311", "A1", "L1210", "L1211", "L1200", "L1310",
    "L1201", "L1111", "L1300", "C0200", "C0010", "L1101", "C0011", "A2", "C0201", "C0300", "C1110", "C1311",
    "L2210", "C1100", "Q", "L2211", "L2110", "C0101", "L2310", "L2111", "L2311", "M0100", "M0301", "C1301",
    "M0000", "M0001", "M1010", "M1011", "M1000", "M1001", "M2200", "M2201", "C0100", "M2100", "M2300", "M2010",
    "M2101", "M2301", "M2011", "M2000", "M2001", "A3", "C0301", "C1010", "C2200", "L3210", "L3211", "L3200",
    "L3110", "L3201", "L3311", "M3310", "C1011", "M3111", "M3100", "M3300", "M3010", "M3101", "M3301", "C2201",
    "P", "C2010", "C2011", "M3011", "M3000", "M3001", "C2300", "C2101", "C2100", "C3310", "R", "C3111", "C3301",
    "C3100", "C3011", "C3010", "R", "C2301", "C3300", "C3101", "R", "F0", "F1", "F2", "F3",
)
STEPS_IN_ORDER = [(w[0], tuple(int(x) for x in w[1:])) for w in ORDER]


def block_order():
    seen = []
    for kind, v in STEPS_IN_ORDER:
        if kind in "LMC":
            b = ((v[1], v[2]), v[3])
            if b not in seen:
                seen.append(b)
        elif kind == "F":
            for b in ((ROOT, 0), (ROOT, 1)):
                if b not in seen:
                    seen.append(b)
    return seen


BLOCKS = block_order()
BLOCK_INDEX = {b: i for i, b in enumerate(BLOCKS)}


def kernel(
    q_ref, ks_ref, vs_ref, kc_ref, vc_ref, len_ref, w_ref, d_ref, u_ref, o_ref,
    q_v, ks_v, vs_v, kc_v, vc_v, w_v, len_v, d_v, u_v, ctx_v, part_v, recv_v, fac_v, proj_v, prcv_v,
    in_sem, w_sem, send_sem, recv_sem, zsend_sem, zrecv_sem, qsend_sem, qrecv_sem, psend_sem, precv_sem,
):
    g = lax.axis_index("group")
    t = lax.axis_index("tensor")
    z, quad = g // 4, g % 4
    y, xh = t // 2, t % 2
    dev = lambda gg, yy, xx: (gg, yy * 2 + xx)
    y_up = dev(g, (y + 1) % 4, xh)
    y_down = dev(g, (y + 3) % 4, xh)
    x_peer = dev(g, y, 1 - xh)
    z_peers = [(((z + k) % 8) * 4 + quad, t) for k in range(1, 8)]
    quad_ids = [(quad + k) % 4 for k in range(1, 4)]
    quad_peers = [(z * 4 + k, t) for k in quad_ids]

    contract = (((1,), (1,)), ((), ()))
    barrier = pltpu.get_barrier_semaphore()
    peers = [y_up, y_down, x_peer] + z_peers + quad_peers
    for p in peers:
        pl.semaphore_signal(barrier, inc=1, device_id=p, device_id_type=MESH)

    def fetch(src, dst, sem):
        c = pltpu.make_async_copy(src, dst, sem)
        c.start()
        return c

    loads = []
    w_loads = []

    def load_rows(k, lo, hi):
        rows = pl.ds(lo, hi - lo)
        loads.append([
            fetch(q_ref.at[:, rows, :], q_v.at[:, rows, :], in_sem.at[k, 0]),
            fetch(kc_ref.at[rows], kc_v.at[rows], in_sem.at[k, 1]),
            fetch(vc_ref.at[rows], vc_v.at[rows], in_sem.at[k, 2]),
        ])

    def load_w(i):
        (r, o), h = BLOCKS[i]
        dest = ((y + 4 - r) % 4) * 2 + ((xh + o) % 2)
        cols = pl.ds(pl.multiple_of(dest * COLS + h * HALF, HALF), HALF)
        w_loads.append(fetch(w_ref.at[:, cols], w_v.at[i], w_sem.at[i]))

    fac_loads = [fetch(d_ref, d_v, in_sem.at[0, 3]), fetch(u_ref, u_v, in_sem.at[0, 4])]
    load_rows(0, 0, 16)
    loads[0] += [
        fetch(ks_ref.at[:, 0:GROUP, :], ks_v.at[:, 0:GROUP, :], in_sem.at[1, 3]),
        fetch(vs_ref.at[:, 0:GROUP, :], vs_v.at[:, 0:GROUP, :], in_sem.at[1, 4]),
        fetch(len_ref, len_v, in_sem.at[0, 5]),
    ]
    load_rows(1, 16, GROUP)
    for i in range(6):
        load_w(i)
    def later_loads():
        load_rows(2, GROUP, ROWS)
        loads[2].extend([
            fetch(ks_ref.at[:, GROUP:, :], ks_v.at[:, GROUP:, :], in_sem.at[2, 3]),
            fetch(vs_ref.at[:, GROUP:, :], vs_v.at[:, GROUP:, :], in_sem.at[2, 4]),
        ])
        for i in range(6, len(BLOCKS)):
            load_w(i)

    waited = set()

    def loaded(k):
        if k not in waited:
            waited.add(k)
            for c in loads[k]:
                c.wait()

    def attention(chunk):
        loaded(0 if chunk == 0 else 2)
        row0, rows = ROW0[chunk], CHUNK_ROWS[chunk]
        g0 = row0 // GROUP * GROUP
        ks_c = ks_v[:, g0:g0 + GROUP, :].reshape(STEPS * GROUP, D)
        vs_c = vs_v[:, g0:g0 + GROUP, :].reshape(STEPS * GROUP, D)
        ones = jnp.ones((STEPS * GROUP, D), BF)
        vs_ext = jnp.concatenate([vs_c, ones], axis=1)
        sub = lax.broadcasted_iota(jnp.int32, (8, 2 * D), 0)
        lane = lax.broadcasted_iota(jnp.int32, (8, 2 * D), 1)

        def sixteen(jj, carry):
            r0 = pl.multiple_of(row0 + jj * 16, 16)
            qf = q_v[:, pl.ds(r0, 16), :].astype(F32)
            outs = []
            for part in range(2):
                qb = jnp.concatenate(
                    [
                        qf[s, part * 8:part * 8 + 8, h * D:(h + 1) * D]
                        for s in range(STEPS)
                        for h in range(HEADS)
                    ],
                    axis=0,
                ).astype(BF)
                rp = r0 + part * 8
                k8 = kc_v[pl.ds(rp, 8)].reshape(8 * CACHE, D)
                v8 = vc_v[pl.ds(rp, 8)].reshape(8 * CACHE, D)
                s1 = lax.dot_general(qb, k8, contract, preferred_element_type=F32)
                s2 = lax.dot_general(qb, ks_c, contract, preferred_element_type=F32)
                lens = jnp.zeros((8, 2 * D), jnp.int32)
                for i in range(8):
                    lens = jnp.where(sub == i, len_v[rp + i], lens)
                ok1 = (lane // CACHE == sub) & (lane % CACHE < lens)
                bias1 = jnp.where(ok1, 0.0, NEG).astype(F32)
                sub2, lane2 = sub[:, :D], lane[:, :D]
                mine = lane2 % GROUP == sub2 + (rp - g0)
                bias2 = jnp.stack(
                    [
                        jnp.where(mine & (lane2 // GROUP <= s), 0.0, NEG).astype(F32)
                        for s in range(STEPS)
                    ]
                )
                s1 = s1.reshape(STEPS * HEADS, 8, 2 * D) + bias1[None]
                s2 = s2.reshape(STEPS, HEADS, 8, D) + bias2[:, None]
                s1 = s1.reshape(STEPS * HEADS * 8, 2 * D)
                s2 = s2.reshape(STEPS * HEADS * 8, D)
                top = jnp.maximum(jnp.maximum(s1[:, :D], s1[:, D:]), s2)
                top = jnp.max(top, axis=1, keepdims=True)
                p1 = jnp.exp2((s1 - top) * EXP2_SCALE).astype(BF)
                p2 = jnp.exp2((s2 - top) * EXP2_SCALE).astype(BF)
                v_ext = jnp.concatenate([v8, jnp.ones((8 * CACHE, D), BF)], axis=1)
                acc = jnp.dot(p1, v_ext, preferred_element_type=F32) + jnp.dot(
                    p2, vs_ext, preferred_element_type=F32
                )
                outs.append(acc[:, :D] / acc[:, D:])
            for s in range(STEPS):
                for h in range(HEADS):
                    i = (s * HEADS + h) * 8
                    tile = jnp.concatenate([outs[0][i:i + 8], outs[1][i:i + 8]], axis=0)
                    at = pl.multiple_of(STEPS * row0 + s * rows + jj * 16, 16)
                    ctx_v[pl.ds(at, 16), h * D:(h + 1) * D] = tile.astype(BF)
            return carry

        if chunk == 0:
            for jj in range(rows // 16):
                loaded(jj)
                sixteen(jj, 0)
                if jj == 0:
                    later_loads()
        else:
            lax.fori_loop(0, rows // 16, sixteen, 0)

    def span(chunk):
        return pl.ds(STEPS * ROW0[chunk], STEPS * CHUNK_ROWS[chunk])

    multiplied = set()
    fetched = set()

    def product(chunk, b):
        if (chunk, b) in multiplied:
            return
        multiplied.add((chunk, b))
        i = BLOCK_INDEX[b]
        if i not in fetched:
            fetched.add(i)
            w_loads[i].wait()
        part_v[i, span(chunk), :] = jnp.dot(
            ctx_v[span(chunk), :], w_v[i], preferred_element_type=F32
        ).astype(BF)

    sends = []

    def target_of(node, parent):
        if node[1] != parent[1]:
            return x_peer
        return y_up if (parent[0] - node[0]) % 4 == 1 else y_down

    def edge_copy(chunk, node, h):
        e = EDGE_INDEX[(node, h)]
        parent = trees_of(chunk)[h][node]
        return pltpu.make_async_remote_copy(
            src_ref=part_v.at[BLOCK_INDEX[(node, h)], span(chunk), :],
            dst_ref=recv_v.at[e, span(chunk), :],
            send_sem=send_sem.at[chunk, e],
            recv_sem=recv_sem.at[chunk, e],
            device_id=target_of(node, parent),
            device_id_type=MESH,
        )

    def send(chunk, node, h):
        c = edge_copy(chunk, node, h)
        c.start()
        sends.append(c)

    def gathered(chunk, node, h):
        total = part_v[BLOCK_INDEX[(node, h)], span(chunk), :].astype(F32)
        for kid in children(trees_of(chunk)[h], node):
            edge_copy(chunk, kid, h).wait_recv()
            total = total + recv_v[EDGE_INDEX[(kid, h)], span(chunk), :].astype(F32)
        return total

    def combine(chunk, node, h):
        i = BLOCK_INDEX[(node, h)]
        part_v[i, span(chunk), :] = gathered(chunk, node, h).astype(BF)
        send(chunk, node, h)

    owner = z == t
    parts = [fac_v.at[quad, pl.ds(0, D), :], fac_v.at[quad, pl.ds(D, 64), :]]
    z_copies = [
        [
            pltpu.make_async_remote_copy(
                src_ref=part, dst_ref=part,
                send_sem=zsend_sem.at[k, i], recv_sem=zrecv_sem.at[i],
                device_id=z_peers[k], device_id_type=MESH,
            )
            for k in range(7)
        ]
        for i, part in enumerate(parts)
    ]
    quad_copies = [
        [
            pltpu.make_async_remote_copy(
                src_ref=part, dst_ref=part,
                send_sem=qsend_sem.at[k, i], recv_sem=qrecv_sem.at[2 - k, i],
                device_id=quad_peers[k], device_id_type=MESH,
            )
            for k in range(3)
        ]
        for i, part in enumerate(parts)
    ]

    def factors_out():
        for c in fac_loads:
            c.wait()

        @pl.when(owner)
        def _():
            fac_v[quad, 0:D, :] = jnp.concatenate([d_v[:, 0:D], d_v[:, D:2 * D]], axis=0).astype(BF)
            fac_v[quad, D:D + 64, :] = u_v[...].astype(BF)
            for c in z_copies[0] + z_copies[1]:
                c.start()

    def factors_quad(i):
        @pl.when(jnp.logical_not(owner))
        def _():
            z_copies[i][0].wait_recv()

        for c in quad_copies[i]:
            c.start()

    def factors_wait(i):
        for c in quad_copies[i]:
            c.wait_recv()

    half_m = STEPS * ROWS // 2
    lane_m = lax.broadcasted_iota(jnp.int32, (half_m, D), 1)

    def project():
        halves = []
        for k in range(2):
            lo = jnp.zeros((half_m, D), F32)
            hi = jnp.zeros((half_m, D), F32)
            ctx = ctx_v[k * half_m:(k + 1) * half_m, :]
            for j in range(4):
                f = fac_v[j, 0:D, :]
                lo = lo + lax.dot_general(
                    ctx[:, 2 * j * D:(2 * j + 1) * D], f, contract, preferred_element_type=F32
                )
                hi = hi + lax.dot_general(
                    ctx[:, (2 * j + 1) * D:(2 * j + 2) * D], f, contract, preferred_element_type=F32
                )
            if k == 0:
                halves.append(lo + pltpu.roll(hi, 64, 1))
            else:
                halves.append(hi + pltpu.roll(lo, 64, 1))
        proj_v[0] = jnp.where(lane_m < 64, halves[0], halves[1]).astype(BF)

    y_pair = dev(g, y + 1 - 2 * (y % 2), xh)
    y_flip = dev(g, 3 - y, xh)
    p_copies = [
        pltpu.make_async_remote_copy(
            src_ref=proj_v.at[k], dst_ref=prcv_v.at[k],
            send_sem=psend_sem.at[k], recv_sem=precv_sem.at[k],
            device_id=p, device_id_type=MESH,
        )
        for k, p in enumerate((x_peer, y_pair, y_flip))
    ]

    def proj_step(k):
        p_copies[k].wait_recv()
        proj_v[k + 1] = (proj_v[k].astype(F32) + prcv_v[k].astype(F32)).astype(BF)
        if k < 2:
            p_copies[k + 1].start()

    def finish(chunk):
        rows, m0 = CHUNK_ROWS[chunk], STEPS * ROW0[chunk]
        m = STEPS * rows
        proj = proj_v[3, pl.ds(m0 % half_m, m), :]
        lane = lax.broadcasted_iota(jnp.int32, (m, D), 1)
        keep = lane < 64 if m0 < half_m else lane >= 64
        proj = jnp.where(keep, proj.astype(F32) * ADAPTER_SCALE, 0.0).astype(BF)
        row_span = pl.ds(ROW0[chunk], rows)
        for h in range(2):
            total = gathered(chunk, ROOT, h)
            for j in range(2):
                u = fac_v[2 * h + j, D:D + 64, :]
                low = jnp.dot(proj, jnp.concatenate([u, u], axis=0), preferred_element_type=F32)
                res = (total[:, j * D:(j + 1) * D] + low).astype(BF)
                o_ref[:, row_span, h * HALF + j * D:h * HALF + (j + 1) * D] = res.reshape(STEPS, rows, D)

    ar_steps = finished = 0
    greeted = False
    for kind, v in STEPS_IN_ORDER:
        if kind in "LO" and not greeted:
            greeted = True
            pl.semaphore_wait(barrier, len(peers))
        if kind == "A":
            attention(v[0])
        elif kind == "O":
            factors_out()
        elif kind in "LMC":
            chunk, node, h = v[0], (v[1], v[2]), v[3]
            product(chunk, (node, h))
            if kind == "L":
                send(chunk, node, h)
            elif kind == "C":
                combine(chunk, node, h)
        elif kind == "F":
            for h in (0, 1):
                product(v[0], (ROOT, h))
            if not finished:
                factors_wait(1)
            finished += 1
            finish(v[0])
        elif kind == "Q":
            factors_quad(0)
        elif kind == "P":
            factors_wait(0)
            project()
            p_copies[0].start()
            factors_quad(1)
        else:
            proj_step(ar_steps)
            ar_steps += 1

    for c in sends:
        c.wait_send()

    @pl.when(owner)
    def _():
        for c in z_copies[0] + z_copies[1]:
            c.wait_send()

    for c in quad_copies[0] + quad_copies[1] + p_copies:
        c.wait_send()


def body(q, ks, vs, kc, vc, lengths, w, d, u):
    hbm = pl.BlockSpec(memory_space=pltpu.HBM)
    dma = pltpu.SemaphoreType.DMA
    return pl.pallas_call(
        kernel,
        out_shape=pltpu.VMEM((STEPS, ROWS, COLS), BF),
        in_specs=[hbm] * 9,
        out_specs=pl.BlockSpec(memory_space=pltpu.VMEM),
        scratch_shapes=[
            pltpu.VMEM((STEPS, ROWS, WIDTH), BF),
            pltpu.VMEM((STEPS, ROWS, D), BF),
            pltpu.VMEM((STEPS, ROWS, D), BF),
            pltpu.VMEM((ROWS, CACHE, D), BF),
            pltpu.VMEM((ROWS, CACHE, D), BF),
            pltpu.VMEM((16, WIDTH, HALF), BF),
            pltpu.SMEM((ROWS,), jnp.int32),
            pltpu.VMEM((64, 256), F32),
            pltpu.VMEM((64, 128), F32),
            pltpu.VMEM((STEPS * ROWS, WIDTH), BF),
            pltpu.VMEM((16, STEPS * ROWS, HALF), BF),
            pltpu.VMEM((14, STEPS * ROWS, HALF), BF),
            pltpu.VMEM((4, D + 64, D), BF),
            pltpu.VMEM((4, STEPS * ROWS // 2, D), BF),
            pltpu.VMEM((3, STEPS * ROWS // 2, D), BF),
            dma((3, 6)),
            dma((16,)),
            dma((CHUNKS, 14)),
            dma((CHUNKS, 14)),
            dma((7, 2)),
            dma((2,)),
            dma((3, 2)),
            dma((3, 2)),
            dma((3,)),
            dma((3,)),
        ],
        compiler_params=pltpu.CompilerParams(
            collective_id=1, has_side_effects=True, vmem_limit_bytes=54 << 20
        ),
        cost_estimate=pl.CostEstimate(
            flops=2 * 512 * 1024 * 4200, bytes_accessed=13 << 20, transcendentals=1 << 20
        ),
        name="attend_project_reduce",
    )(q, ks, vs, kc, vc, lengths, w, d.T, u)


def solution(mesh):
    return jax.shard_map(
        body,
        mesh=mesh,
        in_specs=(
            P(None, "group", "tensor"),
            P(None, "group", "tensor"),
            P(None, "group", "tensor"),
            P("group", None, "tensor"),
            P("group", None, "tensor"),
            P("group"),
            P("tensor", None),
            P("group", None),
            P(None, "group"),
        ),
        out_specs=P(None, "group", "tensor"),
        check_vma=False,
    )
```
